256 devices in a mesh: blk: 64 (over z, x, core), mpo: 4 (over y).
Axes of the slice: x: 4, y: 4, z: 8, core: 2. Of those that a mesh axis runs over, the one named last changes fastest.
Arguments:
- psi: bfloat16 [16, 64, 4, 128, 128], P(None, 'blk'), may hold values from -60 to 60, as said below
- left_env: bfloat16 [64, 32, 128, 128], P('blk'), may hold values from -4 to 4, as said below
- right_env: bfloat16 [64, 32, 128, 128], P('blk'), may hold values from -4 to 4, as said below
- live_count: int32 [64], P('blk'), may hold values from 1 to 4, as said below
- right_sector: int32 [64, 4], P('blk'), may hold values from 0 to 63, as said below
- pattern: int32 [32, 2], P('mpo'), may hold values from 0 to 31, as said below
- term_op: bfloat16 [32, 16, 16], P('mpo'), may hold values from -1 to 1, as said below
Outputs:
- applied: bfloat16 [16, 64, 4, 128, 128], P('mpo', 'blk')
- residual: bfloat16 [16, 64, 4, 128, 128], P('mpo', 'blk')
- energy: float32 [], replicated
The draws below stay inside these ranges and needn't reach their ends.
Inputs may be any that keep to these rules, and one draw needn't show every extreme that they name: psi entries lie between the bounds. `left_env`: environment entries lie between the bounds. `right_env`: environment entries lie between the bounds. `live_count`: some sector has all 4 blocks live. `right_sector`: the right sectors of one left sector l are distinct and lie within 3 of l. pattern[t, 0] lies in 0 to 31; for a term t of group g = t // 8, pattern[t, 1] lies in g * 8 to (g + 1) * 8 - 1. `term_op`: operator entries lie between the bounds.
All inputs are finite; a program needn't handle non-finite values.
Results may differ from the reference program's by a relative error of at most 0.015.
Values may be sent and summed in bfloat16 or wider, within the bound.
No kernel may reach another device: no remote copies, remote signals or barrier semaphores. Data moves between devices by JAX's collectives and lax.ppermute only.
A program may use at most 128 MiB of HBM per device.

```python
import math
import jax
import jax.numpy as jnp
from jax import lax

TILE = 128
PHYS = 16
VBOND = 32
TERM_DEV = 8
SLOTS = 4
HS = 3
SECTORS = 64
VDEV = 8
NTERM = 32
N_MPO = 4


def environment(key, noise):
    first_key, second_key = jax.random.split(jax.random.fold_in(key, 11))
    coupling_factor = jnp.exp(jax.random.uniform(first_key, (SECTORS, VBOND, 1, 1), jnp.float32, -math.log(2.0), math.log(2.0)))
    diagonal = jax.random.uniform(second_key, (SECTORS, VBOND, TILE, 1), jnp.float32, 0.8, 1.2)
    identity = jnp.eye(TILE, dtype=jnp.float32)
    return (coupling_factor * (diagonal * identity + noise * (0.6 / math.sqrt(TILE)))).astype(jnp.bfloat16)


def draw_left_env(key, part):
    key = jax.random.fold_in(key, 2)
    shape = (SECTORS, VBOND, TILE, TILE)
    noise = jax.random.truncated_normal(key, -4.0, 4.0, shape, jnp.float32)
    return environment(key, noise)


def draw_right_env(key, part):
    key = jax.random.fold_in(key, 3)
    shape = (SECTORS, VBOND, TILE, TILE)
    noise = jax.random.truncated_normal(key, -4.0, 4.0, shape, jnp.float32)
    return environment(key, noise)


def draw_psi(key, part):
    key = jax.random.fold_in(key, 1)
    base_key, row_key, column_sector_key = jax.random.split(key, 3)
    shape = (PHYS, SECTORS, SLOTS, TILE, TILE)
    base = jax.random.truncated_normal(base_key, -6.0, 6.0, shape, jnp.float32)
    spread = math.log(3.2)
    row_scale = jnp.exp(jax.random.uniform(row_key, (PHYS, SECTORS, SLOTS, TILE, 1), jnp.float32) * spread)
    column_scale = jnp.exp(jax.random.uniform(column_sector_key, (PHYS, SECTORS, SLOTS, 1, TILE), jnp.float32) * spread)
    sector_index = jnp.arange(SECTORS, dtype=jnp.float32).reshape(1, SECTORS, 1, 1, 1)
    rising = jnp.exp(0.5 * math.log(3.0) * sector_index / max(SECTORS - 1, 1))
    return (0.5 * base * row_scale * column_scale * rising).astype(jnp.bfloat16)


def draw_term_op(key, part):
    key = jax.random.fold_in(key, 4)
    noise_key, diagonal_key = jax.random.split(key)
    shape = (NTERM, PHYS, PHYS)
    noise = jax.random.truncated_normal(noise_key, -5.0, 5.0, shape, jnp.float32)
    diagonal = jax.random.uniform(diagonal_key, (NTERM, PHYS, 1), jnp.float32, 0.5, 1.5) / NTERM
    identity = jnp.eye(PHYS, dtype=jnp.float32)
    return (noise / math.sqrt(PHYS * NTERM) + diagonal * identity).astype(jnp.bfloat16)


def draw_right_sector(key, part):
    key = jax.random.fold_in(key, 5)
    width_all = 2 * HS + 1
    offsets = jnp.arange(width_all, dtype=jnp.int32)
    sector_column = jnp.arange(SECTORS, dtype=jnp.int32)[:, None]
    target = sector_column + offsets[None, :] - HS
    valid = (target >= 0) & (target < SECTORS)
    scores = jax.random.randint(key, (SECTORS, width_all), 0, 4096, jnp.int32) * width_all + offsets[None, :]
    scores = jnp.where(valid, scores, 4096 * width_all + width_all)
    order = jnp.argsort(scores, axis=1, stable=True)
    chosen = order[:, :SLOTS].astype(jnp.int32)
    return (sector_column + chosen - HS).astype(jnp.int32)


def draw_live_count(key, part):
    key = jax.random.fold_in(key, 6)
    count_key, index_key = jax.random.split(key)
    counts = jax.random.randint(count_key, (SECTORS,), 1, SLOTS + 1, jnp.int32)
    chosen = jax.random.randint(index_key, (), 0, SECTORS, jnp.int32)
    return jnp.where(jnp.arange(SECTORS, dtype=jnp.int32) == chosen, SLOTS, counts).astype(jnp.int32)


def draw_pattern(key, part):
    key = jax.random.fold_in(key, 7)
    left_key, right_key = jax.random.split(key)
    term_index = jnp.arange(NTERM, dtype=jnp.int32)
    left_bond = jax.random.randint(left_key, (NTERM,), 0, VBOND, jnp.int32)
    left_bond = jnp.where(term_index == 0, 0, left_bond)
    left_bond = jnp.where(term_index == NTERM - 1, VBOND - 1, left_bond)
    group_start = term_index // TERM_DEV * VDEV
    right_bond = group_start + jax.random.randint(right_key, (NTERM,), 0, VDEV, jnp.int32)
    return jnp.stack([left_bond, right_bond], axis=1).astype(jnp.int32)


def setup_inputs(seed: int = 0) -> dict:
    arg_keys = jax.random.split(jax.random.key(seed), 8)
    return {
        "psi": draw_psi(jax.random.fold_in(arg_keys[7], 71), 0),
        "left_env": draw_left_env(jax.random.fold_in(arg_keys[7], 71), 0),
        "right_env": draw_right_env(jax.random.fold_in(arg_keys[7], 71), 0),
        "live_count": draw_live_count(jax.random.fold_in(arg_keys[7], 71), 0),
        "right_sector": draw_right_sector(jax.random.fold_in(arg_keys[7], 71), 0),
        "pattern": draw_pattern(jax.random.fold_in(arg_keys[7], 71), 0),
        "term_op": draw_term_op(jax.random.fold_in(arg_keys[7], 71), 0),
    }


def group_part(block_psi, term_rows, left_block_rows, onehot, right_rows):
    mixed_operators = jnp.einsum('tpq,qab->tpab', term_rows.astype(jnp.float32), block_psi.astype(jnp.float32), precision=lax.Precision.HIGHEST).astype(jnp.bfloat16)
    left_contraction = jnp.einsum('rxy,rnye->rnxe', left_block_rows.astype(jnp.float32), mixed_operators.astype(jnp.float32), precision=lax.Precision.HIGHEST)
    collected = jnp.einsum('tv,tpab->vpab', onehot, left_contraction, precision=lax.Precision.HIGHEST).astype(jnp.bfloat16)
    return jnp.einsum('vpac,vbc->pab', collected.astype(jnp.float32), right_rows.astype(jnp.float32), precision=lax.Precision.HIGHEST)


def reference(psi, left_env, right_env, live_count, right_sector, pattern, term_op):
    positions = jnp.arange(SLOTS, dtype=jnp.int32)
    live_mask = positions[None, :] < live_count[:, None]
    masked = jnp.where(live_mask[None, :, :, None, None], psi, jnp.zeros_like(psi))
    by_sector = jnp.moveaxis(masked, 1, 0)

    def one_sector(inputs):
        blocks, left_all, sectors = inputs
        output_blocks = []
        for position in range(SLOTS):
            right_environment_all = right_env[sectors[position]]
            summed = jnp.zeros((PHYS, TILE, TILE), jnp.float32)
            for group_index in range(N_MPO):
                rows = pattern[group_index * TERM_DEV:(group_index + 1) * TERM_DEV]
                left_block_rows = left_all[rows[:, 0]]
                local_bond = rows[:, 1] - group_index * VDEV
                onehot = (local_bond[:, None] == jnp.arange(VDEV, dtype=jnp.int32)[None, :]).astype(jnp.float32)
                right_rows = right_environment_all[group_index * VDEV:(group_index + 1) * VDEV]
                term_rows = term_op[group_index * TERM_DEV:(group_index + 1) * TERM_DEV]
                part_value = group_part(blocks[:, position], term_rows, left_block_rows, onehot, right_rows)
                rounded = lax.optimization_barrier(part_value.astype(jnp.bfloat16))
                summed = summed + rounded.astype(jnp.float32)
            output_blocks.append(summed.astype(jnp.bfloat16))
        return jnp.stack(output_blocks, 1)

    applied = lax.map(one_sector, (by_sector, left_env, right_sector))
    applied = jnp.moveaxis(applied, 0, 1)
    masked_values = masked.astype(jnp.float32)
    hamiltonian_values = applied.astype(jnp.float32)
    numerator = jnp.sum(masked_values * hamiltonian_values)
    denominator = jnp.sum(masked_values * masked_values)
    energy = numerator / denominator
    residual = (hamiltonian_values - energy * masked_values).astype(jnp.bfloat16)
    return applied, residual, energy
```

```python
import functools

import jax
import jax.numpy as jnp
from jax import lax
from jax.experimental import pallas as pl
from jax.experimental.pallas import tpu as pltpu
from jax.sharding import PartitionSpec as P

PIECE = ((6, 2, 4, 0, 1, 3, 5), (4, 2, 1, 0, 5, 3, 6))
TERMS = 8
PHYS = 16
SLOTS = 4
TILE = 128
QUARTER = 4


def shift(value, axis, steps):
    count = lax.axis_size(axis)
    return lax.ppermute(value, axis, [(s, (s + steps) % count) for s in range(count)])


def swap(value):
    return lax.ppermute(value, "blk", [(s, s ^ 1) for s in range(lax.axis_size("blk"))])


def neighbours(own):
    count = lax.axis_size("blk")
    odd = lax.axis_index("blk") % 2 == 1
    below = shift(own, "blk", 2)
    above = shift(own, "blk", -2)
    other = swap(own)
    far = jnp.where(odd, below, above)
    far = lax.ppermute(
        far, "blk", [(s, (s + 2) % count if s % 2 else (s - 2) % count) for s in range(count)]
    )
    return own, other, below, above, swap(below), swap(above), swap(far)


def total(value):
    def ring(value, moves):
        moved = [lax.ppermute(value, "blk", [(s, f(s)) for s in range(64)]) for f in moves]
        return functools.reduce(jnp.add, moved, value)

    def along_x(steps):
        return lambda s: (s // 8) * 8 + (s + 2 * steps) % 8

    def along_z(steps):
        return lambda s: (s + 8 * steps) % 64

    value = value + swap(value)
    value = ring(value, [lambda s: s ^ 8])
    value = ring(value, [along_z(2), along_z(4), along_z(6)])
    value = ring(value, [along_x(1), along_x(2), along_x(3)])
    moved = [shift(value, "mpo", d) for d in (1, 2, 3)]
    return functools.reduce(jnp.add, moved, value)


def kernel(scalars, mixed, left, psi, p0, p1, p2, p3, p4, p5, p6, o0, o1, o2, o3, sums, part, right):
    slot = pl.program_id(0)
    pieces = (p0, p1, p2, p3, p4, p5, p6)
    outs = (o0, o1, o2, o3)
    which = scalars[16 + slot]
    for k in range(7):

        @pl.when(which == k)
        def _():
            for t in range(TERMS):
                right[:, t * TILE : (t + 1) * TILE] = pieces[k][scalars[8 + t]]

    for t in range(TERMS):
        factor = left[scalars[t]]
        for p in range(0, PHYS, 4):
            columns = jnp.concatenate([mixed[0, t, p + i] for i in range(4)], 1)
            product = jnp.dot(factor, columns, preferred_element_type=jnp.float32)
            product = product.astype(jnp.bfloat16)
            for i in range(4):
                part[p + i, :, t * TILE : (t + 1) * TILE] = product[:, i * TILE : (i + 1) * TILE]

    numerator = jnp.zeros((TILE, TILE), jnp.float32)
    denominator = jnp.zeros((TILE, TILE), jnp.float32)
    for k in range(4):
        base = lax.rem(scalars[20] + k, 4) * QUARTER
        rows = part[pl.ds(base, QUARTER)].reshape(QUARTER * TILE, TERMS * TILE)
        value = lax.dot_general(
            rows, right[...], (((1,), (1,)), ((), ())), preferred_element_type=jnp.float32
        ).reshape(QUARTER, TILE, TILE)
        outs[k][:, 0] = value.astype(jnp.bfloat16)
        bra = psi[pl.ds(base, QUARTER), 0, 0].astype(jnp.float32)
        numerator += jnp.sum(bra * value, 0)
        denominator += jnp.sum(bra * bra, 0)

    @pl.when(slot == 0)
    def _():
        sums[...] = jnp.zeros_like(sums)

    row = lax.broadcasted_iota(jnp.int32, (8, TILE), 0)
    live = (slot < scalars[21]).astype(jnp.float32)
    numerator = jnp.sum(numerator)
    denominator = jnp.sum(denominator) * (0.25 * live)
    sums[...] += jnp.where(row == 0, numerator, denominator)


def contract(scalars, mixed, left, psi, pieces):
    whole = lambda *shape: pl.BlockSpec(shape, lambda j, s: (0,) * len(shape))
    out = jax.ShapeDtypeStruct((QUARTER, SLOTS, TILE, TILE), jnp.bfloat16)
    return pl.pallas_call(
        kernel,
        grid_spec=pltpu.PrefetchScalarGridSpec(
            num_scalar_prefetch=1,
            grid=(SLOTS,),
            in_specs=[
                pl.BlockSpec((1, TERMS, PHYS, TILE, TILE), lambda j, s: (j, 0, 0, 0, 0)),
                whole(*left.shape),
                pl.BlockSpec((PHYS, 1, 1, TILE, TILE), lambda j, s: (0, 0, j, 0, 0)),
            ]
            + [whole(TERMS, TILE, TILE)] * 7,
            out_specs=[pl.BlockSpec((QUARTER, 1, TILE, TILE), lambda j, s: (0, j, 0, 0))] * 4
            + [whole(8, TILE)],
            scratch_shapes=[
                pltpu.VMEM((PHYS, TILE, TERMS * TILE), jnp.bfloat16),
                pltpu.VMEM((TILE, TERMS * TILE), jnp.bfloat16),
            ],
        ),
        out_shape=[out] * 4 + [jax.ShapeDtypeStruct((8, TILE), jnp.float32)],
        compiler_params=pltpu.CompilerParams(vmem_limit_bytes=48 << 20),
        cost_estimate=pl.CostEstimate(
            flops=4 * SLOTS * TERMS * PHYS * TILE**3, bytes_accessed=24 << 20, transcendentals=0
        ),
    )(scalars, mixed, left, psi, *pieces)


def body(psi, left_env, right_env, live_count, right_sector, pattern, term_op):
    group = lax.axis_index("mpo")
    blk = lax.axis_index("blk")
    own = lax.dynamic_slice_in_dim(right_env[0], group * TERMS, TERMS, 0)
    pieces = neighbours(own)
    live = jnp.arange(SLOTS, dtype=jnp.int32) < live_count[0]
    masked = jnp.where(live[None, None, :, None, None], psi, jnp.zeros_like(psi))
    mixed = jnp.stack(
        [
            jnp.einsum(
                "tpq,qab->tpab", term_op, masked[:, 0, j], preferred_element_type=jnp.float32
            ).astype(jnp.bfloat16)
            for j in range(SLOTS)
        ]
    )
    where = jnp.array(PIECE, jnp.int32)[blk % 2, right_sector[0] - blk + 3]
    scalars = jnp.concatenate(
        [pattern[:, 0], pattern[:, 1] - group * TERMS, where, group[None], live_count]
    ).astype(jnp.int32)
    o0, o1, o2, o3, sums = contract(scalars, mixed, left_env[0], psi, pieces)
    arrived = [shift(value, "mpo", d + 1) for d, value in enumerate((o1, o2, o3))]
    sums = total(sums)
    energy = sums[0, 0] / sums[1, 0]
    summed = functools.reduce(jnp.add, [a.astype(jnp.float32) for a in (o0, *arrived)])
    applied = summed.astype(jnp.bfloat16)
    ket = lax.dynamic_slice_in_dim(masked[:, 0], group * QUARTER, QUARTER, 0)
    residual = (applied.astype(jnp.float32) - energy * ket.astype(jnp.float32)).astype(jnp.bfloat16)
    return applied[:, None], residual[:, None], energy


def solution(mesh):
    placed = (
        P(None, "blk", None, None, None),
        P("blk", None, None, None),
        P("blk", None, None, None),
        P("blk"),
        P("blk", None),
        P("mpo", None),
        P("mpo", None, None),
    )
    return jax.shard_map(
        body,
        mesh=mesh,
        in_specs=placed,
        out_specs=(P("mpo", "blk", None, None, None), P("mpo", "blk", None, None, None), P()),
        check_vma=False,
    )
```

```python
import functools

import jax
import jax.numpy as jnp
from jax import lax
from jax.experimental import pallas as pl
from jax.experimental.pallas import tpu as pltpu
from jax.sharding import PartitionSpec as P

PIECE = ((6, 2, 4, 0, 1, 3, 5), (4, 2, 1, 0, 5, 3, 6))
TERMS = 8
PHYS = 16
SLOTS = 4
TILE = 128
QUARTER = 4
PAD = 136


def shift(value, axis, steps):
    count = lax.axis_size(axis)
    return lax.ppermute(value, axis, [(s, (s + steps) % count) for s in range(count)])


def swap(value):
    return lax.ppermute(value, "blk", [(s, s ^ 1) for s in range(lax.axis_size("blk"))])


def neighbours(own):
    count = lax.axis_size("blk")
    below = shift(own, "blk", 2)
    above = shift(own, "blk", -2)
    far = lax.ppermute(
        own, "blk", [(s, (s + 4) % count if s % 2 else (s - 4) % count) for s in range(count)]
    )
    return swap(own), below, above, far


def left_kernel(first, pattern, live_count, op, left, psi, after, part, token, ket, mixed):
    slot = pl.program_id(0)
    live = slot + first < live_count[0]
    for q in range(PHYS):
        image = psi[q, 0, 0].astype(jnp.float32)
        ket[q * PAD : q * PAD + TILE, :] = jnp.where(live, image, 0.0)
    for a in range(0, TILE, 4):
        columns = [ket[pl.ds(a + i, PHYS, stride=PAD), :].astype(jnp.bfloat16) for i in range(4)]
        product = jnp.dot(op[...], jnp.concatenate(columns, 1), preferred_element_type=jnp.float32)
        for i in range(4):
            mixed[pl.ds(a + i, TERMS * PHYS, stride=PAD), :] = product[:, i * TILE : (i + 1) * TILE]
    for t in range(TERMS):
        factor = left[pattern[t, 0]]
        for p in range(0, PHYS, 4):
            starts = [(t * PHYS + p + i) * PAD for i in range(4)]
            columns = [mixed[start : start + TILE].astype(jnp.bfloat16) for start in starts]
            product = jnp.dot(
                factor, jnp.concatenate(columns, 1), preferred_element_type=jnp.float32
            ).astype(jnp.bfloat16)
            for i in range(4):
                part[slot, p + i, :, t * TILE : (t + 1) * TILE] = product[:, i * TILE : (i + 1) * TILE]
    token[...] = mixed[:8, :]


def whole(*shape):
    return pl.BlockSpec(shape, lambda j, *s: (0,) * len(shape))


def in_hbm(value):
    return pltpu.with_memory_space_constraint(value, pltpu.HBM)


def in_vmem(value):
    return pltpu.with_memory_space_constraint(value, pltpu.VMEM)


def left_product(pattern, live_count, op, left, psi, after, first, count):
    return pl.pallas_call(
        functools.partial(left_kernel, first),
        grid_spec=pltpu.PrefetchScalarGridSpec(
            num_scalar_prefetch=2,
            grid=(count,),
            in_specs=[
                whole(*op.shape),
                whole(*left.shape),
                pl.BlockSpec((PHYS, 1, 1, TILE, TILE), lambda j, *s: (0, 0, j + first, 0, 0)),
                pl.BlockSpec(memory_space=pl.ANY),
            ],
            out_specs=[pl.BlockSpec(memory_space=pltpu.VMEM), whole(8, TILE)],
            scratch_shapes=[
                pltpu.VMEM((PHYS * PAD, TILE), jnp.float32),
                pltpu.VMEM((TERMS * PHYS * PAD, TILE), jnp.float32),
            ],
        ),
        out_shape=[
            pltpu.VMEM((count, PHYS, TILE, TERMS * TILE), jnp.bfloat16),
            jax.ShapeDtypeStruct((8, TILE), jnp.float32),
        ],
        compiler_params=pltpu.CompilerParams(vmem_limit_bytes=20 << 20),
        cost_estimate=pl.CostEstimate(
            flops=12 * count * TERMS * PHYS * TILE**3, bytes_accessed=count << 20, transcendentals=0
        ),
    )(pattern, live_count, op, in_hbm(left), in_hbm(psi), after)


def right_kernel(
    pattern, live_count, right_sector, part_a, part_b, psi, p0, p1, p2, p3, p4, p5, p6,
    o0, o1, o2, o3, ket, sums, right, total,
):
    slot = pl.program_id(0)
    group = lax.axis_index("mpo")
    blk = lax.axis_index("blk")
    pieces = (p0, p1, p2, p3, p4, p5, p6)
    outs = (o0, o1, o2, o3)
    distance = right_sector[0, slot] - blk
    which = jnp.int32(0)
    for d in range(7):
        piece = jnp.where(lax.rem(blk, 2) == 0, PIECE[0][d], PIECE[1][d])
        which = jnp.where(distance == d - 3, piece, which)
    for k in range(7):

        @pl.when(which == k)
        def _():
            for t in range(TERMS):
                right[t * TILE : (t + 1) * TILE, :] = pieces[k][pattern[t, 1] - group * TERMS].T

    @pl.when(slot == 0)
    def _():
        total[...] = jnp.zeros_like(total)

    live = slot < live_count[0]
    own = psi[pl.ds(group * QUARTER, QUARTER), 0, 0]
    ket[:, 0] = jnp.where(live, own, jnp.zeros_like(own))

    def block(part, index):
        numerator = jnp.zeros((TILE, TILE), jnp.float32)
        denominator = jnp.zeros((TILE, TILE), jnp.float32)
        for k in range(4):
            base = lax.rem(group + k, 4) * QUARTER
            rows = part[index, pl.ds(base, QUARTER)].reshape(QUARTER * TILE, TERMS * TILE)
            value = jnp.dot(rows, right[...], preferred_element_type=jnp.float32)
            value = value.reshape(QUARTER, TILE, TILE)
            outs[k][:, 0] = value.astype(jnp.bfloat16)
            bra = psi[pl.ds(base, QUARTER), 0, 0].astype(jnp.float32)
            numerator += jnp.sum(bra * value, 0)
            denominator += jnp.sum(bra * bra, 0)
        total[0] += numerator
        total[1] += denominator * jnp.where(live, 0.25, 0.0)

    split = part_a.shape[0]

    @pl.when(slot < split)
    def _():
        block(part_a, jnp.minimum(slot, split - 1))

    @pl.when(slot >= split)
    def _():
        block(part_b, jnp.maximum(slot - split, 0))

    @pl.when(slot == SLOTS - 1)
    def _():
        lane = lax.broadcasted_iota(jnp.int32, sums.shape, 2)
        sums[...] = jnp.where(lane < TILE // 2, jnp.sum(total[0]), jnp.sum(total[1]))


def right_product(pattern, live_count, right_sector, part_a, part_b, psi, pieces, devices):
    out = jax.ShapeDtypeStruct((QUARTER, SLOTS, TILE, TILE), jnp.bfloat16)
    resident = pl.BlockSpec(memory_space=pltpu.VMEM)
    return pl.pallas_call(
        right_kernel,
        grid_spec=pltpu.PrefetchScalarGridSpec(
            num_scalar_prefetch=3,
            grid=(SLOTS,),
            in_specs=[
                resident,
                resident,
                pl.BlockSpec((PHYS, 1, 1, TILE, TILE), lambda j, *s: (0, 0, j, 0, 0)),
            ]
            + [resident] * 7,
            out_specs=[pl.BlockSpec((QUARTER, 1, TILE, TILE), lambda j, *s: (0, j, 0, 0))] * 5
            + [whole(devices, 1, TILE)],
            scratch_shapes=[
                pltpu.VMEM((TERMS * TILE, TILE), jnp.bfloat16),
                pltpu.VMEM((2, TILE, TILE), jnp.float32),
            ],
        ),
        out_shape=[out] * 5 + [jax.ShapeDtypeStruct((devices, 1, TILE), jnp.float32)],
        compiler_params=pltpu.CompilerParams(vmem_limit_bytes=20 << 20),
        cost_estimate=pl.CostEstimate(
            flops=6 * SLOTS * TERMS * PHYS * TILE**3, bytes_accessed=5 << 20, transcendentals=0
        ),
    )(
        pattern, live_count, right_sector, in_vmem(part_a), in_vmem(part_b), in_hbm(psi),
        *map(in_vmem, pieces),
    )


def last_kernel(sums, o0, r1, r2, r3, ket, applied, residual, energy):
    first = pl.program_id(0) * 2
    lane = lax.broadcasted_iota(jnp.int32, (1, TILE), 1)
    value = jnp.sum(sums[...], 0)
    numerator = jnp.sum(jnp.where(lane == 0, value, 0.0), 1, keepdims=True)
    denominator = jnp.sum(jnp.where(lane == TILE // 2, value, 0.0), 1, keepdims=True)
    quotient = numerator / denominator
    for p in range(QUARTER):
        for j in range(2):
            result = sum(part[p, first + j].astype(jnp.float32) for part in (o0, r1, r2, r3))
            result = result.astype(jnp.bfloat16)
            applied[p, 0, j] = result
            rest = result.astype(jnp.float32) - quotient * ket[p, first + j].astype(jnp.float32)
            residual[p, 0, j] = rest.astype(jnp.bfloat16)
    energy[0, 0] = jnp.sum(quotient)


def last(sums, parts, ket):
    result = pl.BlockSpec((QUARTER, 1, 2, TILE, TILE), lambda j: (0, 0, j, 0, 0))
    out = jax.ShapeDtypeStruct((QUARTER, 1, SLOTS, TILE, TILE), jnp.bfloat16)
    return pl.pallas_call(
        last_kernel,
        grid=(SLOTS // 2,),
        in_specs=[pl.BlockSpec(memory_space=pltpu.VMEM)] * 6,
        out_specs=[result, result, pl.BlockSpec(memory_space=pltpu.SMEM)],
        out_shape=[out, out, jax.ShapeDtypeStruct((1, 1), jnp.float32)],
        compiler_params=pltpu.CompilerParams(vmem_limit_bytes=16 << 20),
        cost_estimate=pl.CostEstimate(flops=1 << 20, bytes_accessed=4 << 20, transcendentals=0),
    )(*map(in_vmem, (sums, *parts, ket)))


def body(psi, left_env, right_env, live_count, right_sector, pattern, term_op):
    group = lax.axis_index("mpo")
    op = term_op.reshape(TERMS * PHYS, PHYS)
    left = left_env[0]
    own = lax.dynamic_slice_in_dim(right_env[0], group * TERMS, TERMS, 0)
    other, below, above, far = neighbours(own)
    part_a, token = left_product(pattern, live_count, op, left, psi, live_count, 0, 3)
    token, below, above, far = lax.optimization_barrier((token, below, above, far))
    crossed = [swap(piece) for piece in (below, above, far)]
    part_b, _ = left_product(pattern, live_count, op, left, psi, token, 3, 1)
    pieces = (own, other, below, above, *crossed)
    devices = lax.axis_size("blk") * lax.axis_size("mpo")
    *parts, ket, sums = right_product(
        pattern, live_count, right_sector, part_a, part_b, psi, pieces, devices
    )
    arrived = [shift(value, "mpo", d + 1) for d, value in enumerate(parts[1:])]
    sums = lax.all_to_all(sums, ("blk", "mpo"), 0, 0, tiled=True)
    applied, residual, energy = last(sums, (parts[0], *arrived), ket)
    return applied, residual, energy[0, 0]


def solution(mesh):
    placed = (
        P(None, "blk", None, None, None),
        P("blk", None, None, None),
        P("blk", None, None, None),
        P("blk"),
        P("blk", None),
        P("mpo", None),
        P("mpo", None, None),
    )
    return jax.shard_map(
        body,
        mesh=mesh,
        in_specs=placed,
        out_specs=(P("mpo", "blk", None, None, None), P("mpo", "blk", None, None, None), P()),
        check_vma=False,
    )
```

```python
import functools

import jax
import jax.numpy as jnp
from jax import lax
from jax.experimental import pallas as pl
from jax.experimental.pallas import tpu as pltpu
from jax.sharding import PartitionSpec as P

PIECE = (
    (6, 3, 5, 0, 1, 2, 4),
    (5, 3, 1, 0, 4, 2, 6),
    (6, 2, 4, 0, 1, 3, 5),
    (4, 2, 1, 0, 5, 3, 6),
)
TERMS = 8
PHYS = 16
SLOTS = 4
TILE = 128
QUARTER = 4


RESIDENT = pl.BlockSpec(memory_space=pltpu.VMEM)


def shift(value, axis, steps):
    count = lax.axis_size(axis)
    return lax.ppermute(value, axis, [(s, (s + steps) % count) for s in range(count)])


def trade(value, partner):
    count = lax.axis_size("blk")
    pairs = [(s, partner(s)) for s in range(count) if 0 <= partner(s) < count]
    return lax.ppermute(value, "blk", pairs)


def swap(value):
    return trade(value, lambda s: s ^ 1)


def passing_kernel(one, two, passed):
    place = lax.rem(lax.axis_index("blk"), 4)
    first = jnp.logical_or(place == 0, place == 3)

    @pl.when(first)
    def _():
        passed[...] = one[...]

    @pl.when(jnp.logical_not(first))
    def _():
        passed[...] = two[...]


def passing(one, two):
    return pl.pallas_call(
        passing_kernel,
        in_specs=[pl.BlockSpec(memory_space=pltpu.VMEM)] * 2,
        out_specs=pl.BlockSpec(memory_space=pltpu.VMEM),
        out_shape=pltpu.VMEM(one.shape, one.dtype),
        compiler_params=pltpu.CompilerParams(vmem_limit_bytes=1 << 20),
    )(in_vmem(one), in_vmem(two))


def whole(*shape):
    return pl.BlockSpec(shape, lambda j, *s: (0,) * len(shape))


def in_hbm(value):
    return pltpu.with_memory_space_constraint(value, pltpu.HBM)


def in_vmem(value):
    return pltpu.with_memory_space_constraint(value, pltpu.VMEM)


def own_kernel(environment, own, done):
    first = lax.axis_index("mpo") * TERMS
    copy = pltpu.make_async_copy(environment.at[0, pl.ds(first, TERMS)], own, done)
    copy.start()
    copy.wait()


def own_rows(environment):
    return pl.pallas_call(
        own_kernel,
        in_specs=[pl.BlockSpec(memory_space=pl.ANY)],
        out_specs=RESIDENT,
        out_shape=pltpu.VMEM((TERMS, TILE, TILE), jnp.bfloat16),
        scratch_shapes=[pltpu.SemaphoreType.DMA],
        compiler_params=pltpu.CompilerParams(vmem_limit_bytes=1 << 20),
    )(in_hbm(environment))


def spread(op, wide):
    rows, columns = wide.shape
    row = lax.broadcasted_iota(jnp.int32, (rows, TERMS * PHYS), 0)
    column = lax.broadcasted_iota(jnp.int32, (rows, TERMS * PHYS), 1)
    pick = (lax.div(row, PHYS) == column).astype(jnp.bfloat16)
    tall = jnp.dot(pick, op, preferred_element_type=jnp.float32).astype(jnp.bfloat16)
    row = lax.broadcasted_iota(jnp.int32, (PHYS, columns), 0)
    column = lax.broadcasted_iota(jnp.int32, (PHYS, columns), 1)
    pick = (lax.div(column, PHYS) == row).astype(jnp.bfloat16)
    full = jnp.dot(tall, pick, preferred_element_type=jnp.float32)
    row = lax.broadcasted_iota(jnp.int32, (rows, columns), 0)
    column = lax.broadcasted_iota(jnp.int32, (rows, columns), 1)
    same = lax.rem(row, PHYS) == lax.rem(column, PHYS)
    wide[...] = jnp.where(same, full, 0.0).astype(jnp.bfloat16)


def left_slot(live, pattern, wide, left, ready, psi, part, slot, mixed):
    for a in range(0, TILE, 32):
        halves = [psi[:, 0, 0, a + h : a + h + 16].reshape(PHYS * 16, TILE) for h in (0, 16)]
        columns = jnp.concatenate(halves, 1)
        columns = jnp.where(live, columns, jnp.zeros_like(columns))
        for m in range(0, TERMS * PHYS, 16):
            product = jnp.dot(
                wide[m * 16 : (m + 16) * 16], columns, preferred_element_type=jnp.float32
            ).astype(jnp.bfloat16)
            for h in (0, 1):
                half = product[:, h * TILE : (h + 1) * TILE].reshape(16, 16, TILE)
                mixed[m : m + 16, a + 16 * h : a + 16 * h + 16, :] = half
    ready()
    for t in range(TERMS):
        factor = left[pattern[0, t]]
        for p in range(0, PHYS, 4):
            columns = jnp.concatenate([mixed[t * PHYS + p + i] for i in range(4)], 1)
            product = jnp.dot(factor, columns, preferred_element_type=jnp.float32)
            product = product.astype(jnp.bfloat16)
            for i in range(4):
                part[slot, p + i, :, t * TILE : (t + 1) * TILE] = product[:, i * TILE : (i + 1) * TILE]


def left_first(pattern, live_count, op, left, psi, part, token, wide, kept, mixed, done):
    slot = pl.program_id(0)
    copy = pltpu.make_async_copy(left, kept, done)

    @pl.when(slot == 0)
    def _():
        copy.start()
        spread(op[...].reshape(TERMS * PHYS, PHYS), wide)
        token[...] = jnp.zeros_like(token)

    def ready():
        pl.when(slot == 0)(copy.wait)

    live = slot < live_count[0]
    left_slot(live, pattern, wide, kept, ready, psi, part, slot, mixed)


def left_second(first, pattern, live_count, wide, left, psi, before, part, mixed):
    slot = pl.program_id(0)
    live = slot + first < live_count[0]
    left_slot(live, pattern, wide, left, lambda: None, psi, part, slot, mixed)


def part_shape(count):
    return pltpu.VMEM((count, PHYS, TILE, TERMS * TILE), jnp.bfloat16)


def left_cost(count):
    return pl.CostEstimate(
        flops=12 * count * TERMS * PHYS * TILE**3, bytes_accessed=count << 20, transcendentals=0
    )


def left_early(pattern, live_count, op, left, psi, count):
    return pl.pallas_call(
        left_first,
        grid_spec=pltpu.PrefetchScalarGridSpec(
            num_scalar_prefetch=2,
            grid=(count,),
            in_specs=[
                whole(*op.shape),
                pl.BlockSpec(memory_space=pl.ANY),
                pl.BlockSpec((PHYS, 1, 1, TILE, TILE), lambda j, *s: (0, 0, j, 0, 0)),
            ],
            out_specs=[RESIDENT, whole(8, TILE), RESIDENT, RESIDENT],
            scratch_shapes=[
                pltpu.VMEM((TERMS * PHYS, TILE, TILE), jnp.bfloat16),
                pltpu.SemaphoreType.DMA,
            ],
        ),
        out_shape=[
            part_shape(count),
            jax.ShapeDtypeStruct((8, TILE), jnp.float32),
            pltpu.VMEM((TERMS * PHYS * 16, PHYS * 16), jnp.bfloat16),
            pltpu.VMEM(left.shape, jnp.bfloat16),
        ],
        compiler_params=pltpu.CompilerParams(vmem_limit_bytes=16 << 20),
        cost_estimate=left_cost(count),
    )(pattern, live_count, in_hbm(op), in_hbm(left), in_hbm(psi))


def left_late(pattern, live_count, wide, left, psi, before, first, count):
    return pl.pallas_call(
        functools.partial(left_second, first),
        grid_spec=pltpu.PrefetchScalarGridSpec(
            num_scalar_prefetch=2,
            grid=(count,),
            in_specs=[
                RESIDENT,
                RESIDENT,
                pl.BlockSpec((PHYS, 1, 1, TILE, TILE), lambda j, *s: (0, 0, j + first, 0, 0)),
                pl.BlockSpec(memory_space=pl.ANY),
            ],
            out_specs=RESIDENT,
            scratch_shapes=[pltpu.VMEM((TERMS * PHYS, TILE, TILE), jnp.bfloat16)],
        ),
        out_shape=part_shape(count),
        compiler_params=pltpu.CompilerParams(vmem_limit_bytes=16 << 20),
        cost_estimate=left_cost(count),
    )(pattern, live_count, in_vmem(wide), in_vmem(left), in_hbm(psi), before)


def right_kernel(
    pattern, live_count, right_sector, part_a, part_b, psi, p0, p1, p2, p3, p4, p5, p6,
    o0, o1, o2, o3, ket, sums, right, total,
):
    slot = pl.program_id(0)
    group = lax.axis_index("mpo")
    blk = lax.axis_index("blk")
    pieces = (p0, p1, p2, p3, p4, p5, p6)
    outs = (o0, o1, o2, o3)
    distance = right_sector[0, slot] - blk
    which = jnp.int32(0)
    for d in range(7):
        for r in range(4):
            here = jnp.logical_and(distance == d - 3, lax.rem(blk, 4) == r)
            which = jnp.where(here, PIECE[r][d], which)
    for k in range(7):

        @pl.when(which == k)
        def _():
            for t in range(TERMS):
                right[t * TILE : (t + 1) * TILE, :] = pieces[k][pattern[1, t] - group * TERMS].T

    @pl.when(slot == 0)
    def _():
        total[...] = jnp.zeros_like(total)

    live = slot < live_count[0]
    own = psi[pl.ds(group * QUARTER, QUARTER), 0, 0]
    ket[:, slot] = jnp.where(live, own, jnp.zeros_like(own))

    def block(part, index):
        numerator = jnp.zeros((TILE, TILE), jnp.float32)
        denominator = jnp.zeros((TILE, TILE), jnp.float32)
        for k in range(4):
            base = lax.rem(group + k, 4) * QUARTER
            rows = part[index, pl.ds(base, QUARTER)].reshape(QUARTER * TILE, TERMS * TILE)
            value = jnp.dot(rows, right[...], preferred_element_type=jnp.float32)
            value = value.reshape(QUARTER, TILE, TILE)
            outs[k][:, slot] = value.astype(jnp.bfloat16)
            bra = psi[pl.ds(base, QUARTER), 0, 0].astype(jnp.float32)
            numerator += jnp.sum(bra * value, 0)
            denominator += jnp.sum(bra * bra, 0)
        total[0] += numerator
        total[1] += denominator * jnp.where(live, 0.25, 0.0)

    split = part_a.shape[0]

    @pl.when(slot < split)
    def _():
        block(part_a, jnp.minimum(slot, split - 1))

    @pl.when(slot >= split)
    def _():
        block(part_b, jnp.maximum(slot - split, 0))

    @pl.when(slot == SLOTS - 1)
    def _():
        lane = lax.broadcasted_iota(jnp.int32, sums.shape, 2)
        sums[...] = jnp.where(lane < TILE // 2, jnp.sum(total[0]), jnp.sum(total[1]))


def right_product(pattern, live_count, right_sector, part_a, part_b, psi, pieces, devices):
    out = pltpu.VMEM((QUARTER, SLOTS, TILE, TILE), jnp.bfloat16)
    return pl.pallas_call(
        right_kernel,
        grid_spec=pltpu.PrefetchScalarGridSpec(
            num_scalar_prefetch=3,
            grid=(SLOTS,),
            in_specs=[
                RESIDENT,
                RESIDENT,
                pl.BlockSpec((PHYS, 1, 1, TILE, TILE), lambda j, *s: (0, 0, j, 0, 0)),
            ]
            + [RESIDENT] * 7,
            out_specs=[RESIDENT] * 6,
            scratch_shapes=[
                pltpu.VMEM((TERMS * TILE, TILE), jnp.bfloat16),
                pltpu.VMEM((2, TILE, TILE), jnp.float32),
            ],
        ),
        out_shape=[out] * 5 + [pltpu.VMEM((devices, 1, TILE), jnp.float32)],
        compiler_params=pltpu.CompilerParams(vmem_limit_bytes=12 << 20),
        cost_estimate=pl.CostEstimate(
            flops=6 * SLOTS * TERMS * PHYS * TILE**3, bytes_accessed=5 << 20, transcendentals=0
        ),
    )(
        pattern, live_count, right_sector, in_vmem(part_a), in_vmem(part_b), in_hbm(psi),
        *map(in_vmem, pieces),
    )


def last_kernel(sums, o0, r1, r2, r3, ket, applied, residual, energy):
    first = pl.program_id(0) * 2
    lane = lax.broadcasted_iota(jnp.int32, (1, TILE), 1)
    value = jnp.sum(sums[...], 0)
    numerator = jnp.sum(jnp.where(lane == 0, value, 0.0), 1, keepdims=True)
    denominator = jnp.sum(jnp.where(lane == TILE // 2, value, 0.0), 1, keepdims=True)
    quotient = numerator / denominator
    for p in range(QUARTER):
        for j in range(2):
            result = sum(part[p, first + j].astype(jnp.float32) for part in (o0, r1, r2, r3))
            result = result.astype(jnp.bfloat16)
            applied[p, 0, j] = result
            rest = result.astype(jnp.float32) - quotient * ket[p, first + j].astype(jnp.float32)
            residual[p, 0, j] = rest.astype(jnp.bfloat16)
    energy[0, 0] = jnp.sum(quotient)


def last(sums, parts, ket):
    result = pl.BlockSpec((QUARTER, 1, 2, TILE, TILE), lambda j: (0, 0, j, 0, 0))
    out = jax.ShapeDtypeStruct((QUARTER, 1, SLOTS, TILE, TILE), jnp.bfloat16)
    return pl.pallas_call(
        last_kernel,
        grid=(SLOTS // 2,),
        in_specs=[pl.BlockSpec(memory_space=pltpu.VMEM)] * 6,
        out_specs=[result, result, pl.BlockSpec(memory_space=pltpu.SMEM)],
        out_shape=[out, out, jax.ShapeDtypeStruct((1, 1), jnp.float32)],
        compiler_params=pltpu.CompilerParams(vmem_limit_bytes=16 << 20),
        cost_estimate=pl.CostEstimate(flops=1 << 20, bytes_accessed=4 << 20, transcendentals=0),
    )(*map(in_vmem, (sums, *parts, ket)))


def body(psi, left_env, right_env, live_count, right_sector, pattern, term_op):
    pattern = pattern.T
    own = own_rows(right_env)
    one = trade(own, lambda s: s ^ 2)
    two = trade(own, lambda s: s + 2 if s % 4 > 1 else s - 2)
    other = swap(own)
    part_a, token, wide, left = left_early(pattern, live_count, term_op, left_env[0], psi, 3)
    token, one, two = lax.optimization_barrier((token, one, two))
    far = trade(passing(one, two), lambda s: s + 1 if s % 2 else s - 1)
    pieces = (own, other, one, two, swap(one), swap(two), far)
    part_b = left_late(pattern, live_count, wide, left, psi, token, 3, 1)
    devices = lax.axis_size("blk") * lax.axis_size("mpo")
    *parts, ket, sums = right_product(
        pattern, live_count, right_sector, part_a, part_b, psi, pieces, devices
    )
    arrived = [shift(value, "mpo", d + 1) for d, value in enumerate(parts[1:])]
    sums = lax.all_to_all(sums, ("blk", "mpo"), 0, 0, tiled=True)
    applied, residual, energy = last(sums, (parts[0], *arrived), ket)
    return applied, residual, energy[0, 0]


def solution(mesh):
    placed = (
        P(None, "blk", None, None, None),
        P("blk", None, None, None),
        P("blk", None, None, None),
        P("blk"),
        P("blk", None),
        P("mpo", None),
        P("mpo", None, None),
    )
    return jax.shard_map(
        body,
        mesh=mesh,
        in_specs=placed,
        out_specs=(P("mpo", "blk", None, None, None), P("mpo", "blk", None, None, None), P()),
        check_vma=False,
    )
```

```python
import functools

import jax
import jax.numpy as jnp
from jax import lax
from jax.experimental import pallas as pl
from jax.experimental.pallas import tpu as pltpu
from jax.sharding import PartitionSpec as P

PIECE = (
    (6, 3, 5, 0, 1, 2, 4),
    (5, 3, 1, 0, 4, 2, 6),
    (6, 2, 4, 0, 1, 3, 5),
    (4, 2, 1, 0, 5, 3, 6),
)
TERMS = 8
PHYS = 16
SLOTS = 4
TILE = 128
QUARTER = 4


RESIDENT = pl.BlockSpec(memory_space=pltpu.VMEM)


def shift(value, axis, steps):
    count = lax.axis_size(axis)
    return lax.ppermute(value, axis, [(s, (s + steps) % count) for s in range(count)])


def trade(value, partner):
    count = lax.axis_size("blk")
    pairs = [(s, partner(s)) for s in range(count) if 0 <= partner(s) < count]
    return lax.ppermute(value, "blk", pairs)


def swap(value):
    return trade(value, lambda s: s ^ 1)


def passing_kernel(one, two, passed):
    place = lax.rem(lax.axis_index("blk"), 4)
    first = jnp.logical_or(place == 0, place == 3)

    @pl.when(first)
    def _():
        passed[...] = one[...]

    @pl.when(jnp.logical_not(first))
    def _():
        passed[...] = two[...]


def passing(one, two):
    return pl.pallas_call(
        passing_kernel,
        in_specs=[pl.BlockSpec(memory_space=pltpu.VMEM)] * 2,
        out_specs=pl.BlockSpec(memory_space=pltpu.VMEM),
        out_shape=pltpu.VMEM(one.shape, one.dtype),
        compiler_params=pltpu.CompilerParams(vmem_limit_bytes=1 << 20),
    )(in_vmem(one), in_vmem(two))


def whole(*shape):
    return pl.BlockSpec(shape, lambda j, *s: (0,) * len(shape))


def in_hbm(value):
    return pltpu.with_memory_space_constraint(value, pltpu.HBM)


def in_vmem(value):
    return pltpu.with_memory_space_constraint(value, pltpu.VMEM)


def own_kernel(environment, own, done):
    first = lax.axis_index("mpo") * TERMS
    copy = pltpu.make_async_copy(environment.at[0, pl.ds(first, TERMS)], own, done)
    copy.start()
    copy.wait()


def own_rows(environment):
    return pl.pallas_call(
        own_kernel,
        in_specs=[pl.BlockSpec(memory_space=pl.ANY)],
        out_specs=RESIDENT,
        out_shape=pltpu.VMEM((TERMS, TILE, TILE), jnp.bfloat16),
        scratch_shapes=[pltpu.SemaphoreType.DMA],
        compiler_params=pltpu.CompilerParams(vmem_limit_bytes=1 << 20),
    )(in_hbm(environment))


def spread(op, wide):
    rows, columns = wide.shape
    row = lax.broadcasted_iota(jnp.int32, (rows, TERMS * PHYS), 0)
    column = lax.broadcasted_iota(jnp.int32, (rows, TERMS * PHYS), 1)
    pick = (lax.div(row, PHYS) == column).astype(jnp.bfloat16)
    tall = jnp.dot(pick, op, preferred_element_type=jnp.float32).astype(jnp.bfloat16)
    row = lax.broadcasted_iota(jnp.int32, (PHYS, columns), 0)
    column = lax.broadcasted_iota(jnp.int32, (PHYS, columns), 1)
    pick = (lax.div(column, PHYS) == row).astype(jnp.bfloat16)
    full = jnp.dot(tall, pick, preferred_element_type=jnp.float32)
    row = lax.broadcasted_iota(jnp.int32, (rows, columns), 0)
    column = lax.broadcasted_iota(jnp.int32, (rows, columns), 1)
    same = lax.rem(row, PHYS) == lax.rem(column, PHYS)
    wide[...] = jnp.where(same, full, 0.0).astype(jnp.bfloat16)


def left_slot(live, pattern, wide, left, ready, psi, part, slot, mixed):
    for a in range(0, TILE, 32):
        halves = [psi[:, 0, 0, a + h : a + h + 16].reshape(PHYS * 16, TILE) for h in (0, 16)]
        columns = jnp.concatenate(halves, 1)
        columns = jnp.where(live, columns, jnp.zeros_like(columns))
        for m in range(0, TERMS * PHYS, 16):
            product = jnp.dot(
                wide[m * 16 : (m + 16) * 16], columns, preferred_element_type=jnp.float32
            ).astype(jnp.bfloat16)
            for h in (0, 1):
                half = product[:, h * TILE : (h + 1) * TILE].reshape(16, 16, TILE)
                mixed[m : m + 16, a + 16 * h : a + 16 * h + 16, :] = half
    ready()
    for t in range(TERMS):
        factor = left[pattern[0, t]]
        for p in range(0, PHYS, 4):
            columns = jnp.concatenate([mixed[t * PHYS + p + i] for i in range(4)], 1)
            product = jnp.dot(factor, columns, preferred_element_type=jnp.float32)
            product = product.astype(jnp.bfloat16)
            for i in range(4):
                part[slot, p + i, :, t * TILE : (t + 1) * TILE] = product[:, i * TILE : (i + 1) * TILE]


def left_first(pattern, live_count, op, left, psi, part, token, wide, kept, mixed, done):
    slot = pl.program_id(0)
    copy = pltpu.make_async_copy(left, kept, done)

    @pl.when(slot == 0)
    def _():
        copy.start()
        spread(op[...].reshape(TERMS * PHYS, PHYS), wide)
        token[...] = jnp.zeros_like(token)

    def ready():
        pl.when(slot == 0)(copy.wait)

    live = slot < live_count[0]
    left_slot(live, pattern, wide, kept, ready, psi, part, slot, mixed)


def left_second(first, pattern, live_count, wide, left, psi, before, part, mixed):
    slot = pl.program_id(0)
    live = slot + first < live_count[0]
    left_slot(live, pattern, wide, left, lambda: None, psi, part, slot, mixed)


def part_shape(count):
    return pltpu.VMEM((count, PHYS, TILE, TERMS * TILE), jnp.bfloat16)


def left_cost(count):
    return pl.CostEstimate(
        flops=12 * count * TERMS * PHYS * TILE**3, bytes_accessed=count << 20, transcendentals=0
    )


def left_early(pattern, live_count, op, left, psi, count):
    return pl.pallas_call(
        left_first,
        grid_spec=pltpu.PrefetchScalarGridSpec(
            num_scalar_prefetch=2,
            grid=(count,),
            in_specs=[
                whole(*op.shape),
                pl.BlockSpec(memory_space=pl.ANY),
                pl.BlockSpec((PHYS, 1, 1, TILE, TILE), lambda j, *s: (0, 0, j, 0, 0)),
            ],
            out_specs=[RESIDENT, whole(8, TILE), RESIDENT, RESIDENT],
            scratch_shapes=[
                pltpu.VMEM((TERMS * PHYS, TILE, TILE), jnp.bfloat16),
                pltpu.SemaphoreType.DMA,
            ],
        ),
        out_shape=[
            part_shape(count),
            jax.ShapeDtypeStruct((8, TILE), jnp.float32),
            pltpu.VMEM((TERMS * PHYS * 16, PHYS * 16), jnp.bfloat16),
            pltpu.VMEM(left.shape, jnp.bfloat16),
        ],
        compiler_params=pltpu.CompilerParams(vmem_limit_bytes=16 << 20),
        cost_estimate=left_cost(count),
    )(pattern, live_count, in_hbm(op), in_hbm(left), in_hbm(psi))


def left_late(pattern, live_count, wide, left, psi, before, first, count):
    return pl.pallas_call(
        functools.partial(left_second, first),
        grid_spec=pltpu.PrefetchScalarGridSpec(
            num_scalar_prefetch=2,
            grid=(count,),
            in_specs=[
                RESIDENT,
                RESIDENT,
                pl.BlockSpec((PHYS, 1, 1, TILE, TILE), lambda j, *s: (0, 0, j + first, 0, 0)),
                pl.BlockSpec(memory_space=pl.ANY),
            ],
            out_specs=RESIDENT,
            scratch_shapes=[pltpu.VMEM((TERMS * PHYS, TILE, TILE), jnp.bfloat16)],
        ),
        out_shape=part_shape(count),
        compiler_params=pltpu.CompilerParams(vmem_limit_bytes=16 << 20),
        cost_estimate=left_cost(count),
    )(pattern, live_count, in_vmem(wide), in_vmem(left), in_hbm(psi), before)


def right_kernel(
    pattern, live_count, right_sector, part_a, part_b, psi, p0, p1, p2, p3, p4, p5, p6,
    o0, o1, o2, o3, ket, sums, chosen, right, total, done,
):
    slot = pl.program_id(0)
    group = lax.axis_index("mpo")
    blk = lax.axis_index("blk")
    pieces = (p0, p1, p2, p3, p4, p5, p6)
    outs = (o0, o1, o2, o3)

    def choose(j):
        distance = right_sector[0, j] - blk
        which = jnp.int32(0)
        for d in range(7):
            for r in range(4):
                here = jnp.logical_and(distance == d - 3, lax.rem(blk, 4) == r)
                which = jnp.where(here, PIECE[r][d], which)
        for k in range(7):
            copy = pltpu.make_async_copy(pieces[k], chosen.at[j], done.at[j])
            pl.when(which == k)(copy.start)

    def arrive(j):
        pltpu.make_async_copy(p0, chosen.at[j], done.at[j]).wait()

    def turn(j):
        for t in range(TERMS):
            block = chosen[j, pattern[1, t] - group * TERMS]
            right[lax.rem(j, 2), t * TILE : (t + 1) * TILE, :] = block.T

    @pl.when(slot == 0)
    def _():
        for j in range(SLOTS):
            choose(j)
        total[...] = jnp.zeros_like(total)
        arrive(0)
        turn(0)

    following = jnp.minimum(slot + 1, SLOTS - 1)
    pl.when(slot < SLOTS - 1)(lambda: arrive(following))
    live = slot < live_count[0]
    own = psi[pl.ds(group * QUARTER, QUARTER), 0, 0]
    ket[:, slot] = jnp.where(live, own, jnp.zeros_like(own))

    def block(part, index):
        numerator = jnp.zeros((TILE, TILE), jnp.float32)
        denominator = jnp.zeros((TILE, TILE), jnp.float32)
        for k in range(4):
            base = lax.rem(group + k, 4) * QUARTER
            rows = part[index, pl.ds(base, QUARTER)].reshape(QUARTER * TILE, TERMS * TILE)
            here = right[lax.rem(slot, 2)]
            value = jnp.dot(rows, here, preferred_element_type=jnp.float32)
            value = value.reshape(QUARTER, TILE, TILE)
            outs[k][:, slot] = value.astype(jnp.bfloat16)
            bra = psi[pl.ds(base, QUARTER), 0, 0].astype(jnp.float32)
            numerator += jnp.sum(bra * value, 0)
            denominator += jnp.sum(bra * bra, 0)
        total[0] += numerator
        total[1] += denominator * jnp.where(live, 0.25, 0.0)
        turn(following)

    split = part_a.shape[0]
    pl.when(slot < split)(lambda: block(part_a, jnp.minimum(slot, split - 1)))
    pl.when(slot >= split)(lambda: block(part_b, jnp.maximum(slot - split, 0)))

    @pl.when(slot == SLOTS - 1)
    def _():
        lane = lax.broadcasted_iota(jnp.int32, sums.shape, 2)
        sums[...] = jnp.where(lane < TILE // 2, jnp.sum(total[0]), jnp.sum(total[1]))


def right_product(pattern, live_count, right_sector, part_a, part_b, psi, pieces, devices):
    out = pltpu.VMEM((QUARTER, SLOTS, TILE, TILE), jnp.bfloat16)
    return pl.pallas_call(
        right_kernel,
        grid_spec=pltpu.PrefetchScalarGridSpec(
            num_scalar_prefetch=3,
            grid=(SLOTS,),
            in_specs=[
                RESIDENT,
                RESIDENT,
                pl.BlockSpec((PHYS, 1, 1, TILE, TILE), lambda j, *s: (0, 0, j, 0, 0)),
            ]
            + [RESIDENT] * 7,
            out_specs=[RESIDENT] * 6,
            scratch_shapes=[
                pltpu.VMEM((SLOTS, TERMS, TILE, TILE), jnp.bfloat16),
                pltpu.VMEM((2, TERMS * TILE, TILE), jnp.bfloat16),
                pltpu.VMEM((2, TILE, TILE), jnp.float32),
                pltpu.SemaphoreType.DMA((SLOTS,)),
            ],
        ),
        out_shape=[out] * 5 + [pltpu.VMEM((devices, 1, TILE), jnp.float32)],
        compiler_params=pltpu.CompilerParams(vmem_limit_bytes=12 << 20),
        cost_estimate=pl.CostEstimate(
            flops=6 * SLOTS * TERMS * PHYS * TILE**3, bytes_accessed=5 << 20, transcendentals=0
        ),
    )(
        pattern, live_count, right_sector, in_vmem(part_a), in_vmem(part_b), in_hbm(psi),
        *map(in_vmem, pieces),
    )


def last_kernel(sums, o0, r1, r2, r3, ket, applied, residual, energy):
    first = pl.program_id(0) * 2
    lane = lax.broadcasted_iota(jnp.int32, (1, TILE), 1)
    value = jnp.sum(sums[...], 0)
    numerator = jnp.sum(jnp.where(lane == 0, value, 0.0), 1, keepdims=True)
    denominator = jnp.sum(jnp.where(lane == TILE // 2, value, 0.0), 1, keepdims=True)
    quotient = numerator / denominator
    for p in range(QUARTER):
        for j in range(2):
            result = sum(part[p, first + j].astype(jnp.float32) for part in (o0, r1, r2, r3))
            result = result.astype(jnp.bfloat16)
            applied[p, 0, j] = result
            rest = result.astype(jnp.float32) - quotient * ket[p, first + j].astype(jnp.float32)
            residual[p, 0, j] = rest.astype(jnp.bfloat16)
    energy[0, 0] = jnp.sum(quotient)


def last(sums, parts, ket):
    result = pl.BlockSpec((QUARTER, 1, 2, TILE, TILE), lambda j: (0, 0, j, 0, 0))
    out = jax.ShapeDtypeStruct((QUARTER, 1, SLOTS, TILE, TILE), jnp.bfloat16)
    return pl.pallas_call(
        last_kernel,
        grid=(SLOTS // 2,),
        in_specs=[pl.BlockSpec(memory_space=pltpu.VMEM)] * 6,
        out_specs=[result, result, pl.BlockSpec(memory_space=pltpu.SMEM)],
        out_shape=[out, out, jax.ShapeDtypeStruct((1, 1), jnp.float32)],
        compiler_params=pltpu.CompilerParams(vmem_limit_bytes=16 << 20),
        cost_estimate=pl.CostEstimate(flops=1 << 20, bytes_accessed=4 << 20, transcendentals=0),
    )(*map(in_vmem, (sums, *parts, ket)))


def body(psi, left_env, right_env, live_count, right_sector, pattern, term_op):
    pattern = in_hbm(pattern.T)
    own = own_rows(right_env)
    one = trade(own, lambda s: s ^ 2)
    two = trade(own, lambda s: s + 2 if s % 4 > 1 else s - 2)
    other = swap(own)
    part_a, token, wide, left = left_early(pattern, live_count, term_op, left_env[0], psi, 2)
    token, one, two = lax.optimization_barrier((token, one, two))
    far = trade(passing(one, two), lambda s: s + 1 if s % 2 else s - 1)
    pieces = (own, other, one, two, swap(one), swap(two), far)
    part_b = left_late(pattern, live_count, wide, left, psi, token, 2, 2)
    devices = lax.axis_size("blk") * lax.axis_size("mpo")
    *parts, ket, sums = right_product(
        pattern, live_count, right_sector, part_a, part_b, psi, pieces, devices
    )
    arrived = [shift(value, "mpo", d + 1) for d, value in enumerate(parts[1:])]
    sums = lax.all_to_all(sums, ("blk", "mpo"), 0, 0, tiled=True)
    applied, residual, energy = last(sums, (parts[0], *arrived), ket)
    return applied, residual, energy[0, 0]


def solution(mesh):
    placed = (
        P(None, "blk", None, None, None),
        P("blk", None, None, None),
        P("blk", None, None, None),
        P("blk"),
        P("blk", None),
        P("mpo", None),
        P("mpo", None, None),
    )
    return jax.shard_map(
        body,
        mesh=mesh,
        in_specs=placed,
        out_specs=(P("mpo", "blk", None, None, None), P("mpo", "blk", None, None, None), P()),
        check_vma=False,
    )
```

```python
import functools

import jax
import jax.numpy as jnp
from jax import lax
from jax.experimental import pallas as pl
from jax.experimental.pallas import tpu as pltpu
from jax.sharding import PartitionSpec as P

PIECE = (
    (6, 3, 5, 0, 1, 2, 4),
    (5, 3, 1, 0, 4, 2, 6),
    (6, 2, 4, 0, 1, 3, 5),
    (4, 2, 1, 0, 5, 3, 6),
)
TERMS = 8
PHYS = 16
SLOTS = 4
TILE = 128
QUARTER = 4


RESIDENT = pl.BlockSpec(memory_space=pltpu.VMEM)


def shift(value, axis, steps):
    count = lax.axis_size(axis)
    return lax.ppermute(value, axis, [(s, (s + steps) % count) for s in range(count)])


def trade(value, partner):
    count = lax.axis_size("blk")
    pairs = [(s, partner(s)) for s in range(count) if 0 <= partner(s) < count]
    return lax.ppermute(value, "blk", pairs)


def swap(value):
    return trade(value, lambda s: s ^ 1)


def passing_kernel(one, two, passed):
    place = lax.rem(lax.axis_index("blk"), 4)
    first = jnp.logical_or(place == 0, place == 3)

    @pl.when(first)
    def _():
        passed[...] = one[...]

    @pl.when(jnp.logical_not(first))
    def _():
        passed[...] = two[...]


def passing(one, two):
    return pl.pallas_call(
        passing_kernel,
        in_specs=[pl.BlockSpec(memory_space=pltpu.VMEM)] * 2,
        out_specs=pl.BlockSpec(memory_space=pltpu.VMEM),
        out_shape=pltpu.VMEM(one.shape, one.dtype),
        compiler_params=pltpu.CompilerParams(vmem_limit_bytes=1 << 20),
    )(in_vmem(one), in_vmem(two))


def whole(*shape):
    return pl.BlockSpec(shape, lambda j, *s: (0,) * len(shape))


def in_hbm(value):
    return pltpu.with_memory_space_constraint(value, pltpu.HBM)


def in_vmem(value):
    return pltpu.with_memory_space_constraint(value, pltpu.VMEM)


def own_kernel(environment, own, done):
    first = lax.axis_index("mpo") * TERMS
    copy = pltpu.make_async_copy(environment.at[0, pl.ds(first, TERMS)], own, done)
    copy.start()
    copy.wait()


def own_rows(environment):
    return pl.pallas_call(
        own_kernel,
        in_specs=[pl.BlockSpec(memory_space=pl.ANY)],
        out_specs=RESIDENT,
        out_shape=pltpu.VMEM((TERMS, TILE, TILE), jnp.bfloat16),
        scratch_shapes=[pltpu.SemaphoreType.DMA],
        compiler_params=pltpu.CompilerParams(vmem_limit_bytes=1 << 20),
    )(in_hbm(environment))


def spread(op, wide):
    rows, columns = wide.shape
    row = lax.broadcasted_iota(jnp.int32, (rows, TERMS * PHYS), 0)
    column = lax.broadcasted_iota(jnp.int32, (rows, TERMS * PHYS), 1)
    pick = (lax.div(row, PHYS) == column).astype(jnp.bfloat16)
    tall = jnp.dot(pick, op, preferred_element_type=jnp.float32).astype(jnp.bfloat16)
    row = lax.broadcasted_iota(jnp.int32, (PHYS, columns), 0)
    column = lax.broadcasted_iota(jnp.int32, (PHYS, columns), 1)
    pick = (lax.div(column, PHYS) == row).astype(jnp.bfloat16)
    full = jnp.dot(tall, pick, preferred_element_type=jnp.float32)
    row = lax.broadcasted_iota(jnp.int32, (rows, columns), 0)
    column = lax.broadcasted_iota(jnp.int32, (rows, columns), 1)
    same = lax.rem(row, PHYS) == lax.rem(column, PHYS)
    wide[...] = jnp.where(same, full, 0.0).astype(jnp.bfloat16)


def left_slot(pattern, wide, left, ready, psi, part, slot, mixed):
    for a in range(0, TILE, 32):
        halves = [psi[:, 0, 0, a + h : a + h + 16].reshape(PHYS * 16, TILE) for h in (0, 16)]
        columns = jnp.concatenate(halves, 1)
        for m in range(0, TERMS * PHYS, 16):
            product = jnp.dot(
                wide[m * 16 : (m + 16) * 16], columns, preferred_element_type=jnp.float32
            ).astype(jnp.bfloat16)
            for h in (0, 1):
                half = product[:, h * TILE : (h + 1) * TILE].reshape(16, 16, TILE)
                mixed[m : m + 16, a + 16 * h : a + 16 * h + 16, :] = half
    ready()
    for t in range(TERMS):
        factor = left[pattern[0, t]]
        for p in range(0, PHYS, 4):
            columns = jnp.concatenate([mixed[t * PHYS + p + i] for i in range(4)], 1)
            product = jnp.dot(factor, columns, preferred_element_type=jnp.float32)
            product = product.astype(jnp.bfloat16)
            for i in range(4):
                part[slot, p + i, :, t * TILE : (t + 1) * TILE] = product[:, i * TILE : (i + 1) * TILE]


def left_first(pattern, live_count, op, left, psi, part, token, wide, kept, mixed, done):
    slot = pl.program_id(0)
    copy = pltpu.make_async_copy(left, kept, done)

    @pl.when(slot == 0)
    def _():
        copy.start()
        spread(op[...].reshape(TERMS * PHYS, PHYS), wide)
        token[...] = jnp.zeros_like(token)

    def ready():
        pl.when(slot == 0)(copy.wait)

    @pl.when(jnp.logical_or(slot == 0, slot < live_count[0]))
    def _():
        left_slot(pattern, wide, kept, ready, psi, part, slot, mixed)


def left_second(first, pattern, live_count, wide, left, psi, before, part, mixed):
    slot = pl.program_id(0)

    @pl.when(slot + first < live_count[0])
    def _():
        left_slot(pattern, wide, left, lambda: None, psi, part, slot, mixed)


def part_shape(count):
    return pltpu.VMEM((count, PHYS, TILE, TERMS * TILE), jnp.bfloat16)


def left_cost(count):
    return pl.CostEstimate(
        flops=12 * count * TERMS * PHYS * TILE**3, bytes_accessed=count << 20, transcendentals=0
    )


def left_early(pattern, live_count, op, left, psi, count):
    return pl.pallas_call(
        left_first,
        grid_spec=pltpu.PrefetchScalarGridSpec(
            num_scalar_prefetch=2,
            grid=(count,),
            in_specs=[
                whole(*op.shape),
                pl.BlockSpec(memory_space=pl.ANY),
                pl.BlockSpec((PHYS, 1, 1, TILE, TILE), lambda j, *s: (0, 0, j, 0, 0)),
            ],
            out_specs=[RESIDENT, whole(8, TILE), RESIDENT, RESIDENT],
            scratch_shapes=[
                pltpu.VMEM((TERMS * PHYS, TILE, TILE), jnp.bfloat16),
                pltpu.SemaphoreType.DMA,
            ],
        ),
        out_shape=[
            part_shape(count),
            jax.ShapeDtypeStruct((8, TILE), jnp.float32),
            pltpu.VMEM((TERMS * PHYS * 16, PHYS * 16), jnp.bfloat16),
            pltpu.VMEM(left.shape, jnp.bfloat16),
        ],
        compiler_params=pltpu.CompilerParams(vmem_limit_bytes=16 << 20),
        cost_estimate=left_cost(count),
    )(pattern, live_count, in_hbm(op), in_hbm(left), in_hbm(psi))


def left_late(pattern, live_count, wide, left, psi, before, first, count):
    return pl.pallas_call(
        functools.partial(left_second, first),
        grid_spec=pltpu.PrefetchScalarGridSpec(
            num_scalar_prefetch=2,
            grid=(count,),
            in_specs=[
                RESIDENT,
                RESIDENT,
                pl.BlockSpec((PHYS, 1, 1, TILE, TILE), lambda j, *s: (0, 0, j + first, 0, 0)),
                pl.BlockSpec(memory_space=pl.ANY),
            ],
            out_specs=RESIDENT,
            scratch_shapes=[pltpu.VMEM((TERMS * PHYS, TILE, TILE), jnp.bfloat16)],
        ),
        out_shape=part_shape(count),
        compiler_params=pltpu.CompilerParams(vmem_limit_bytes=16 << 20),
        cost_estimate=left_cost(count),
    )(pattern, live_count, in_vmem(wide), in_vmem(left), in_hbm(psi), before)


def right_kernel(
    pattern, live_count, right_sector, part_a, part_b, psi, p0, p1, p2, p3, p4, p5, p6,
    o0, o1, o2, o3, ket, sums, chosen, right, total, done,
):
    slot = pl.program_id(0)
    group = lax.axis_index("mpo")
    blk = lax.axis_index("blk")
    pieces = (p0, p1, p2, p3, p4, p5, p6)
    outs = (o0, o1, o2, o3)

    def choose(j):
        distance = right_sector[0, j] - blk
        which = jnp.int32(0)
        for d in range(7):
            for r in range(4):
                here = jnp.logical_and(distance == d - 3, lax.rem(blk, 4) == r)
                which = jnp.where(here, PIECE[r][d], which)
        for k in range(7):
            copy = pltpu.make_async_copy(pieces[k], chosen.at[j], done.at[j])
            pl.when(which == k)(copy.start)

    def arrive(j):
        pltpu.make_async_copy(p0, chosen.at[j], done.at[j]).wait()

    def turn(j):
        for t in range(TERMS):
            block = chosen[j, pattern[1, t] - group * TERMS]
            right[lax.rem(j, 2), t * TILE : (t + 1) * TILE, :] = block.T

    @pl.when(slot == 0)
    def _():
        for j in range(SLOTS):
            choose(j)
        total[...] = jnp.zeros_like(total)
        arrive(0)
        turn(0)

    following = jnp.minimum(slot + 1, SLOTS - 1)
    pl.when(slot < SLOTS - 1)(lambda: arrive(following))
    live = slot < live_count[0]
    own = psi[pl.ds(group * QUARTER, QUARTER), 0, 0]
    ket[:, slot] = jnp.where(live, own, jnp.zeros_like(own))

    def block(part, index):
        numerator = jnp.zeros((TILE, TILE), jnp.float32)
        denominator = jnp.zeros((TILE, TILE), jnp.float32)
        for k in range(4):
            base = lax.rem(group + k, 4) * QUARTER
            rows = part[index, pl.ds(base, QUARTER)].reshape(QUARTER * TILE, TERMS * TILE)
            here = right[lax.rem(slot, 2)]
            value = jnp.dot(rows, here, preferred_element_type=jnp.float32)
            value = value.reshape(QUARTER, TILE, TILE)
            outs[k][:, slot] = value.astype(jnp.bfloat16)
            bra = psi[pl.ds(base, QUARTER), 0, 0].astype(jnp.float32)
            numerator += jnp.sum(bra * value, 0)
            denominator += jnp.sum(bra * bra, 0)
        total[0] += numerator
        total[1] += denominator * 0.25
        turn(following)

    split = part_a.shape[0]
    pl.when(jnp.logical_and(live, slot < split))(lambda: block(part_a, jnp.minimum(slot, split - 1)))
    pl.when(jnp.logical_and(live, slot >= split))(lambda: block(part_b, jnp.maximum(slot - split, 0)))

    @pl.when(jnp.logical_not(live))
    def _():
        for out in outs:
            out[:, slot] = jnp.zeros((QUARTER, TILE, TILE), jnp.bfloat16)

    @pl.when(slot == SLOTS - 1)
    def _():
        lane = lax.broadcasted_iota(jnp.int32, sums.shape, 2)
        sums[...] = jnp.where(lane < TILE // 2, jnp.sum(total[0]), jnp.sum(total[1]))


def right_product(pattern, live_count, right_sector, part_a, part_b, psi, pieces, devices):
    out = pltpu.VMEM((QUARTER, SLOTS, TILE, TILE), jnp.bfloat16)
    return pl.pallas_call(
        right_kernel,
        grid_spec=pltpu.PrefetchScalarGridSpec(
            num_scalar_prefetch=3,
            grid=(SLOTS,),
            in_specs=[
                RESIDENT,
                RESIDENT,
                pl.BlockSpec((PHYS, 1, 1, TILE, TILE), lambda j, *s: (0, 0, j, 0, 0)),
            ]
            + [RESIDENT] * 7,
            out_specs=[RESIDENT] * 6,
            scratch_shapes=[
                pltpu.VMEM((SLOTS, TERMS, TILE, TILE), jnp.bfloat16),
                pltpu.VMEM((2, TERMS * TILE, TILE), jnp.bfloat16),
                pltpu.VMEM((2, TILE, TILE), jnp.float32),
                pltpu.SemaphoreType.DMA((SLOTS,)),
            ],
        ),
        out_shape=[out] * 5 + [pltpu.VMEM((devices, 1, TILE), jnp.float32)],
        compiler_params=pltpu.CompilerParams(vmem_limit_bytes=12 << 20),
        cost_estimate=pl.CostEstimate(
            flops=6 * SLOTS * TERMS * PHYS * TILE**3, bytes_accessed=5 << 20, transcendentals=0
        ),
    )(
        pattern, live_count, right_sector, in_vmem(part_a), in_vmem(part_b), in_hbm(psi),
        *map(in_vmem, pieces),
    )


def last_kernel(sums, o0, r1, r2, r3, ket, applied, residual, energy):
    first = pl.program_id(0) * 2
    lane = lax.broadcasted_iota(jnp.int32, (1, TILE), 1)
    value = jnp.sum(sums[...], 0)
    numerator = jnp.sum(jnp.where(lane == 0, value, 0.0), 1, keepdims=True)
    denominator = jnp.sum(jnp.where(lane == TILE // 2, value, 0.0), 1, keepdims=True)
    quotient = numerator / denominator
    for p in range(QUARTER):
        for j in range(2):
            result = sum(part[p, first + j].astype(jnp.float32) for part in (o0, r1, r2, r3))
            result = result.astype(jnp.bfloat16)
            applied[p, 0, j] = result
            rest = result.astype(jnp.float32) - quotient * ket[p, first + j].astype(jnp.float32)
            residual[p, 0, j] = rest.astype(jnp.bfloat16)
    energy[0, 0] = jnp.sum(quotient)


def last(sums, parts, ket):
    result = pl.BlockSpec((QUARTER, 1, 2, TILE, TILE), lambda j: (0, 0, j, 0, 0))
    out = jax.ShapeDtypeStruct((QUARTER, 1, SLOTS, TILE, TILE), jnp.bfloat16)
    return pl.pallas_call(
        last_kernel,
        grid=(SLOTS // 2,),
        in_specs=[pl.BlockSpec(memory_space=pltpu.VMEM)] * 6,
        out_specs=[result, result, pl.BlockSpec(memory_space=pltpu.SMEM)],
        out_shape=[out, out, jax.ShapeDtypeStruct((1, 1), jnp.float32)],
        compiler_params=pltpu.CompilerParams(vmem_limit_bytes=16 << 20),
        cost_estimate=pl.CostEstimate(flops=1 << 20, bytes_accessed=4 << 20, transcendentals=0),
    )(*map(in_vmem, (sums, *parts, ket)))


def body(psi, left_env, right_env, live_count, right_sector, pattern, term_op):
    pattern = in_hbm(pattern.T)
    own = own_rows(right_env)
    one = trade(own, lambda s: s ^ 2)
    two = trade(own, lambda s: s + 2 if s % 4 > 1 else s - 2)
    other = swap(own)
    part_a, token, wide, left = left_early(pattern, live_count, term_op, left_env[0], psi, 2)
    token, one, two = lax.optimization_barrier((token, one, two))
    far = trade(passing(one, two), lambda s: s + 1 if s % 2 else s - 1)
    pieces = (own, other, one, two, swap(one), swap(two), far)
    part_b = left_late(pattern, live_count, wide, left, psi, token, 2, 2)
    devices = lax.axis_size("blk") * lax.axis_size("mpo")
    *parts, ket, sums = right_product(
        pattern, live_count, right_sector, part_a, part_b, psi, pieces, devices
    )
    arrived = [shift(value, "mpo", d + 1) for d, value in enumerate(parts[1:])]
    sums = lax.all_to_all(sums, ("blk", "mpo"), 0, 0, tiled=True)
    applied, residual, energy = last(sums, (parts[0], *arrived), ket)
    return applied, residual, energy[0, 0]


def solution(mesh):
    placed = (
        P(None, "blk", None, None, None),
        P("blk", None, None, None),
        P("blk", None, None, None),
        P("blk"),
        P("blk", None),
        P("mpo", None),
        P("mpo", None, None),
    )
    return jax.shard_map(
        body,
        mesh=mesh,
        in_specs=placed,
        out_specs=(P("mpo", "blk", None, None, None), P("mpo", "blk", None, None, None), P()),
        check_vma=False,
    )
```

```python
import functools

import jax
import jax.numpy as jnp
from jax import lax
from jax.experimental import pallas as pl
from jax.experimental.pallas import tpu as pltpu
from jax.sharding import PartitionSpec as P

PIECE = (
    (6, 3, 5, 0, 1, 2, 4),
    (5, 3, 1, 0, 4, 2, 6),
    (6, 2, 4, 0, 1, 3, 5),
    (4, 2, 1, 0, 5, 3, 6),
)
TERMS = 8
PHYS = 16
SLOTS = 4
TILE = 128
QUARTER = 4


RESIDENT = pl.BlockSpec(memory_space=pltpu.VMEM)


def shift(value, axis, steps):
    count = lax.axis_size(axis)
    return lax.ppermute(value, axis, [(s, (s + steps) % count) for s in range(count)])


def trade(value, partner):
    count = lax.axis_size("blk")
    pairs = [(s, partner(s)) for s in range(count) if 0 <= partner(s) < count]
    return lax.ppermute(value, "blk", pairs)


def swap(value):
    return trade(value, lambda s: s ^ 1)


def passing_kernel(one, two, passed):
    place = lax.rem(lax.axis_index("blk"), 4)
    first = jnp.logical_or(place == 0, place == 3)

    @pl.when(first)
    def _():
        passed[...] = one[...]

    @pl.when(jnp.logical_not(first))
    def _():
        passed[...] = two[...]


def passing(one, two):
    return pl.pallas_call(
        passing_kernel,
        in_specs=[pl.BlockSpec(memory_space=pltpu.VMEM)] * 2,
        out_specs=pl.BlockSpec(memory_space=pltpu.VMEM),
        out_shape=pltpu.VMEM(one.shape, one.dtype),
        compiler_params=pltpu.CompilerParams(vmem_limit_bytes=1 << 20),
    )(in_vmem(one), in_vmem(two))


def whole(*shape):
    return pl.BlockSpec(shape, lambda j, *s: (0,) * len(shape))


def in_hbm(value):
    return pltpu.with_memory_space_constraint(value, pltpu.HBM)


def in_vmem(value):
    return pltpu.with_memory_space_constraint(value, pltpu.VMEM)


def own_kernel(environment, own, done):
    first = lax.axis_index("mpo") * TERMS
    copy = pltpu.make_async_copy(environment.at[0, pl.ds(first, TERMS)], own, done)
    copy.start()
    copy.wait()


def own_rows(environment):
    return pl.pallas_call(
        own_kernel,
        in_specs=[pl.BlockSpec(memory_space=pl.ANY)],
        out_specs=RESIDENT,
        out_shape=pltpu.VMEM((TERMS, TILE, TILE), jnp.bfloat16),
        scratch_shapes=[pltpu.SemaphoreType.DMA],
        compiler_params=pltpu.CompilerParams(vmem_limit_bytes=1 << 20),
    )(in_hbm(environment))


def spread(op, wide):
    rows, columns = wide.shape
    row = lax.broadcasted_iota(jnp.int32, (rows, TERMS * PHYS), 0)
    column = lax.broadcasted_iota(jnp.int32, (rows, TERMS * PHYS), 1)
    pick = (lax.div(row, PHYS) == column).astype(jnp.bfloat16)
    tall = jnp.dot(pick, op, preferred_element_type=jnp.float32).astype(jnp.bfloat16)
    row = lax.broadcasted_iota(jnp.int32, (PHYS, columns), 0)
    column = lax.broadcasted_iota(jnp.int32, (PHYS, columns), 1)
    pick = (lax.div(column, PHYS) == row).astype(jnp.bfloat16)
    full = jnp.dot(tall, pick, preferred_element_type=jnp.float32)
    row = lax.broadcasted_iota(jnp.int32, (rows, columns), 0)
    column = lax.broadcasted_iota(jnp.int32, (rows, columns), 1)
    same = lax.rem(row, PHYS) == lax.rem(column, PHYS)
    wide[...] = jnp.where(same, full, 0.0).astype(jnp.bfloat16)


def left_slot(pattern, wide, left, ready, psi, part, slot, mixed):
    for a in range(0, TILE, 32):
        halves = [psi[:, 0, 0, a + h : a + h + 16].reshape(PHYS * 16, TILE) for h in (0, 16)]
        columns = jnp.concatenate(halves, 1)
        for m in range(0, TERMS * PHYS, 16):
            product = jnp.dot(
                wide[m * 16 : (m + 16) * 16], columns, preferred_element_type=jnp.float32
            ).astype(jnp.bfloat16)
            for h in (0, 1):
                half = product[:, h * TILE : (h + 1) * TILE].reshape(16, 16, TILE)
                mixed[m : m + 16, a + 16 * h : a + 16 * h + 16, :] = half
    ready()
    for t in range(TERMS):
        factor = left[pattern[0, t]]
        for p in range(0, PHYS, 4):
            columns = jnp.concatenate([mixed[t * PHYS + p + i] for i in range(4)], 1)
            product = jnp.dot(factor, columns, preferred_element_type=jnp.float32)
            product = product.astype(jnp.bfloat16)
            for i in range(4):
                part[slot, p + i, :, t * TILE : (t + 1) * TILE] = product[:, i * TILE : (i + 1) * TILE]


def left_first(pattern, live_count, op, left, psi, part, token, wide, kept, mixed, done):
    slot = pl.program_id(0)
    copy = pltpu.make_async_copy(left, kept, done)

    @pl.when(slot == 0)
    def _():
        copy.start()
        spread(op[...].reshape(TERMS * PHYS, PHYS), wide)
        token[...] = jnp.zeros_like(token)

    def ready():
        pl.when(slot == 0)(copy.wait)

    @pl.when(jnp.logical_or(slot == 0, slot < live_count[0]))
    def _():
        left_slot(pattern, wide, kept, ready, psi, part, slot, mixed)


def left_second(first, pattern, live_count, wide, left, psi, before, part, mixed):
    slot = pl.program_id(0)

    @pl.when(slot + first < live_count[0])
    def _():
        left_slot(pattern, wide, left, lambda: None, psi, part, slot, mixed)


def part_shape(count):
    return pltpu.VMEM((count, PHYS, TILE, TERMS * TILE), jnp.bfloat16)


def left_cost(count):
    return pl.CostEstimate(
        flops=12 * count * TERMS * PHYS * TILE**3, bytes_accessed=count << 20, transcendentals=0
    )


def left_early(pattern, live_count, op, left, psi, count):
    return pl.pallas_call(
        left_first,
        grid_spec=pltpu.PrefetchScalarGridSpec(
            num_scalar_prefetch=2,
            grid=(count,),
            in_specs=[
                whole(*op.shape),
                pl.BlockSpec(memory_space=pl.ANY),
                pl.BlockSpec((PHYS, 1, 1, TILE, TILE), lambda j, *s: (0, 0, j, 0, 0)),
            ],
            out_specs=[RESIDENT, whole(8, TILE), RESIDENT, RESIDENT],
            scratch_shapes=[
                pltpu.VMEM((TERMS * PHYS, TILE, TILE), jnp.bfloat16),
                pltpu.SemaphoreType.DMA,
            ],
        ),
        out_shape=[
            part_shape(count),
            jax.ShapeDtypeStruct((8, TILE), jnp.float32),
            pltpu.VMEM((TERMS * PHYS * 16, PHYS * 16), jnp.bfloat16),
            pltpu.VMEM(left.shape, jnp.bfloat16),
        ],
        compiler_params=pltpu.CompilerParams(vmem_limit_bytes=16 << 20),
        cost_estimate=left_cost(count),
    )(pattern, live_count, in_hbm(op), in_hbm(left), in_hbm(psi))


def left_late(pattern, live_count, wide, left, psi, before, first, count):
    return pl.pallas_call(
        functools.partial(left_second, first),
        grid_spec=pltpu.PrefetchScalarGridSpec(
            num_scalar_prefetch=2,
            grid=(count,),
            in_specs=[
                RESIDENT,
                RESIDENT,
                pl.BlockSpec((PHYS, 1, 1, TILE, TILE), lambda j, *s: (0, 0, j + first, 0, 0)),
                pl.BlockSpec(memory_space=pl.ANY),
            ],
            out_specs=RESIDENT,
            scratch_shapes=[pltpu.VMEM((TERMS * PHYS, TILE, TILE), jnp.bfloat16)],
        ),
        out_shape=part_shape(count),
        compiler_params=pltpu.CompilerParams(vmem_limit_bytes=16 << 20),
        cost_estimate=left_cost(count),
    )(pattern, live_count, in_vmem(wide), in_vmem(left), in_hbm(psi), before)


def right_kernel(
    pattern, live_count, right_sector, part_a, part_b, psi, p0, p1, p2, p3, p4, p5, p6,
    o0, o1, o2, o3, ket, sums, chosen, right, total, done,
):
    slot = pl.program_id(0)
    group = lax.axis_index("mpo")
    blk = lax.axis_index("blk")
    pieces = (p0, p1, p2, p3, p4, p5, p6)
    outs = (o0, o1, o2, o3)

    def choose(j):
        distance = right_sector[0, j] - blk
        which = jnp.int32(0)
        for d in range(7):
            for r in range(4):
                here = jnp.logical_and(distance == d - 3, lax.rem(blk, 4) == r)
                which = jnp.where(here, PIECE[r][d], which)
        for k in range(7):
            copy = pltpu.make_async_copy(pieces[k], chosen.at[j], done.at[j])
            pl.when(which == k)(copy.start)

    def arrive(j):
        pltpu.make_async_copy(p0, chosen.at[j], done.at[j]).wait()

    def turn(j):
        for t in range(TERMS):
            block = chosen[j, pattern[1, t] - group * TERMS]
            right[lax.rem(j, 2), t * TILE : (t + 1) * TILE, :] = block.T

    @pl.when(slot == 0)
    def _():
        for j in range(SLOTS):
            choose(j)
        total[...] = jnp.zeros_like(total)
        arrive(0)
        turn(0)

    following = jnp.minimum(slot + 1, SLOTS - 1)
    pl.when(slot < SLOTS - 1)(lambda: arrive(following))
    live = slot < live_count[0]
    own = psi[pl.ds(group * QUARTER, QUARTER), 0, 0]
    ket[:, slot] = jnp.where(live, own, jnp.zeros_like(own))

    def block(part, index):
        numerator = jnp.zeros((TILE, TILE), jnp.float32)
        denominator = jnp.zeros((TILE, TILE), jnp.float32)
        for k in range(4):
            base = lax.rem(group + k, 4) * QUARTER
            rows = part[index, pl.ds(base, QUARTER)].reshape(QUARTER * TILE, TERMS * TILE)
            here = right[lax.rem(slot, 2)]
            value = jnp.dot(rows, here, preferred_element_type=jnp.float32)
            value = value.reshape(QUARTER, TILE, TILE)
            outs[k][:, slot] = value.astype(jnp.bfloat16)
            bra = psi[pl.ds(base, QUARTER), 0, 0].astype(jnp.float32)
            numerator += jnp.sum(bra * value, 0)
            denominator += jnp.sum(bra * bra, 0)
        total[0] += numerator
        total[1] += denominator * 0.25
        turn(following)

    split = part_a.shape[0]
    pl.when(jnp.logical_and(live, slot < split))(lambda: block(part_a, jnp.minimum(slot, split - 1)))
    pl.when(jnp.logical_and(live, slot >= split))(lambda: block(part_b, jnp.maximum(slot - split, 0)))

    @pl.when(jnp.logical_not(live))
    def _():
        for out in outs:
            out[:, slot] = jnp.zeros((QUARTER, TILE, TILE), jnp.bfloat16)

    @pl.when(slot == SLOTS - 1)
    def _():
        lane = lax.broadcasted_iota(jnp.int32, sums.shape, 2)
        sums[...] = jnp.where(lane < TILE // 2, jnp.sum(total[0]), jnp.sum(total[1]))


def right_product(pattern, live_count, right_sector, part_a, part_b, psi, pieces, devices):
    out = pltpu.VMEM((QUARTER, SLOTS, TILE, TILE), jnp.bfloat16)
    return pl.pallas_call(
        right_kernel,
        grid_spec=pltpu.PrefetchScalarGridSpec(
            num_scalar_prefetch=3,
            grid=(SLOTS,),
            in_specs=[
                RESIDENT,
                RESIDENT,
                pl.BlockSpec((PHYS, 1, 1, TILE, TILE), lambda j, *s: (0, 0, j, 0, 0)),
            ]
            + [RESIDENT] * 7,
            out_specs=[RESIDENT] * 6,
            scratch_shapes=[
                pltpu.VMEM((SLOTS, TERMS, TILE, TILE), jnp.bfloat16),
                pltpu.VMEM((2, TERMS * TILE, TILE), jnp.bfloat16),
                pltpu.VMEM((2, TILE, TILE), jnp.float32),
                pltpu.SemaphoreType.DMA((SLOTS,)),
            ],
        ),
        out_shape=[out] * 5 + [pltpu.VMEM((devices, 1, TILE), jnp.float32)],
        compiler_params=pltpu.CompilerParams(vmem_limit_bytes=12 << 20),
        cost_estimate=pl.CostEstimate(
            flops=6 * SLOTS * TERMS * PHYS * TILE**3, bytes_accessed=5 << 20, transcendentals=0
        ),
    )(
        pattern, live_count, right_sector, in_vmem(part_a), in_vmem(part_b), in_hbm(psi),
        *map(in_vmem, pieces),
    )


def last_kernel(sums, o0, r1, r2, r3, ket, applied, residual, energy, quotient):
    slot = pl.program_id(0)

    @pl.when(slot == 0)
    def _():
        lane = lax.broadcasted_iota(jnp.int32, (1, TILE), 1)
        value = jnp.sum(sums[...], 0)
        numerator = jnp.sum(jnp.where(lane == 0, value, 0.0), 1, keepdims=True)
        denominator = jnp.sum(jnp.where(lane == TILE // 2, value, 0.0), 1, keepdims=True)
        quotient[...] = jnp.broadcast_to(numerator / denominator, quotient.shape)
        energy[0, 0] = jnp.sum(numerator / denominator)

    for p in range(QUARTER):
        result = sum(part[p, slot].astype(jnp.float32) for part in (o0, r1, r2, r3))
        result = result.astype(jnp.bfloat16)
        applied[p, 0, 0] = result
        rest = result.astype(jnp.float32) - quotient[...] * ket[p, slot].astype(jnp.float32)
        residual[p, 0, 0] = rest.astype(jnp.bfloat16)


def last(sums, parts, ket):
    result = pl.BlockSpec((QUARTER, 1, 1, TILE, TILE), lambda j: (0, 0, j, 0, 0))
    out = jax.ShapeDtypeStruct((QUARTER, 1, SLOTS, TILE, TILE), jnp.bfloat16)
    return pl.pallas_call(
        last_kernel,
        grid=(SLOTS,),
        in_specs=[RESIDENT] * 6,
        out_specs=[result, result, pl.BlockSpec(memory_space=pltpu.SMEM)],
        out_shape=[out, out, jax.ShapeDtypeStruct((1, 1), jnp.float32)],
        scratch_shapes=[pltpu.VMEM((1, TILE), jnp.float32)],
        compiler_params=pltpu.CompilerParams(vmem_limit_bytes=16 << 20),
        cost_estimate=pl.CostEstimate(flops=1 << 20, bytes_accessed=4 << 20, transcendentals=0),
    )(*map(in_vmem, (sums, *parts, ket)))


def body(psi, left_env, right_env, live_count, right_sector, pattern, term_op):
    pattern = in_hbm(pattern.T)
    own = own_rows(right_env)
    one = trade(own, lambda s: s ^ 2)
    two = trade(own, lambda s: s + 2 if s % 4 > 1 else s - 2)
    other = swap(own)
    part_a, token, wide, left = left_early(pattern, live_count, term_op, left_env[0], psi, 2)
    token, one, two = lax.optimization_barrier((token, one, two))
    far = trade(passing(one, two), lambda s: s + 1 if s % 2 else s - 1)
    pieces = (own, other, one, two, swap(one), swap(two), far)
    part_b = left_late(pattern, live_count, wide, left, psi, token, 2, 2)
    devices = lax.axis_size("blk") * lax.axis_size("mpo")
    *parts, ket, sums = right_product(
        pattern, live_count, right_sector, part_a, part_b, psi, pieces, devices
    )
    arrived = [shift(value, "mpo", d + 1) for d, value in enumerate(parts[1:])]
    sums = lax.all_to_all(sums, ("blk", "mpo"), 0, 0, tiled=True)
    applied, residual, energy = last(sums, (parts[0], *arrived), ket)
    return applied, residual, energy[0, 0]


def solution(mesh):
    placed = (
        P(None, "blk", None, None, None),
        P("blk", None, None, None),
        P("blk", None, None, None),
        P("blk"),
        P("blk", None),
        P("mpo", None),
        P("mpo", None, None),
    )
    return jax.shard_map(
        body,
        mesh=mesh,
        in_specs=placed,
        out_specs=(P("mpo", "blk", None, None, None), P("mpo", "blk", None, None, None), P()),
        check_vma=False,
    )
```
